128 devices in a mesh: dp: 16 (over z_lo, x, core), tensor: 8 (over y, z_hi).
Axes of the slice: x: 4, y: 4, z: 4 (z_hi: 2, z_lo: 2; z = z_hi * 2 + z_lo), core: 2. Of those that a mesh axis runs over, the one named last changes fastest.
Arguments:
- tokens: bfloat16 [16, 512, 4096], P('dp', 'tensor'), may hold values from -6 to 6
- norm_gain: float32 [16, 4096], P('dp'), may hold values from 0.5 to 1.5
- w_query: bfloat16 [16, 4096, 4096], P('dp', None, 'tensor'), may hold values from -6 to 6
- key_weight: bfloat16 [16, 4096, 1024], P('dp', None, 'tensor'), may hold values from -6 to 6
- value_weight: bfloat16 [16, 4096, 1024], P('dp', None, 'tensor'), may hold values from -6 to 6
- w_out: bfloat16 [16, 4096, 4096], P('dp', 'tensor'), may hold values from -6 to 6
- doc_ids: int32 [16, 512], P('dp'), may hold values from 0 to 3, never falling along the last dimension, each value on 1 to 256 neighbouring positions
- upstream: bfloat16 [16, 512, 4096], P('dp', 'tensor'), may hold values from -6 to 6
- step_count: int32 [1], replicated, may hold values from 0 to 999
Outputs:
- mixed_query: bfloat16 [16, 4096, 4096], P('dp', None, 'tensor')
- mixed_key: bfloat16 [16, 4096, 1024], P('dp', None, 'tensor')
- mixed_value: bfloat16 [16, 4096, 1024], P('dp', None, 'tensor')
- mixed_out: bfloat16 [16, 4096, 4096], P('dp', 'tensor')
- mixed_gain: float32 [16, 4096], P('dp')
- input_grad: bfloat16 [16, 512, 4096], P('dp', 'tensor')
The draws below stay inside these ranges and needn't reach their ends.
All inputs are finite; a program needn't handle non-finite values.
Results may differ from the reference program's by a relative error of at most 0.022.
Values may be sent and summed in bfloat16 or wider, within the bound.
No kernel may reach another device: no remote copies, remote signals or barrier semaphores. Data moves between devices by JAX's collectives and lax.ppermute only.
A program may use at most 128 MiB of HBM per device.

```python
import math
import jax
import jax.numpy as jnp
import numpy as np
from jax import lax

MODEL_WIDTH = 4096
HEAD = 128
TOK = 512
REPLICA_COUNT = 16
HQ = 4096
KEY_FEATURES = 1024
N_DP = 16


def block_levels(own_key, extent, shards, low, top_value):
    gain, own = 1.0, jax.random.fold_in(own_key, 6)
    for position, blocks in shards:
        draws = jnp.exp(jax.random.uniform(jax.random.fold_in(own, position), (blocks,), jnp.float32, low / len(shards), top_value / len(shards)))
        gain = gain * jnp.repeat(draws, extent[position] // blocks).reshape([-1 if axis == position else 1 for axis in range(len(extent))])
    return gain


def profile(count, total, reach, slope):
    weights = [(1 << 20) // math.isqrt(grade ** slope) + 1 for grade in range(2, count + 1)]
    rest, holding = total - reach - (count - 1), [1] * (count - 1)
    while rest > 0:
        free = [i for i in range(count - 1) if holding[i] < reach]
        mass, left = sum([weights[i] for i in free]), rest
        for i in free:
            more = min(reach - holding[i], max(1, left * weights[i] // mass), rest)
            holding[i] = holding[i] + more
            rest = rest - more
    return np.array([reach] + holding)


def ragged(stream_key, count, total, reach, skew):
    if count == 2:
        one = jax.random.randint(stream_key, (), max(1, total - reach), min(reach, total - 1) + 1)
        return jnp.stack([one, total - one])
    sizes = jnp.asarray(profile(count, total, reach, skew), jnp.int32)
    pairs = (count - 1) // 2
    donor, receiver = sizes[1:1 + 2 * pairs:2], sizes[2:2 + 2 * pairs:2]
    slack = jnp.minimum(donor - 1, reach - receiver)
    passed = jax.random.randint(jax.random.fold_in(stream_key, 1), (pairs,), 0, 1 << 20) % (slack + 1)
    sizes = sizes.at[1:1 + 2 * pairs:2].set(donor - passed).at[2:2 + 2 * pairs:2].set(receiver + passed)
    return sizes[jax.random.permutation(jax.random.fold_in(stream_key, 2), count)]


def gaussian(key, extent, spread, limit, split=(), kind=jnp.bfloat16):
    level = block_levels(key, extent, split, -0.22, 0.18) if split else 1.0
    values = jax.random.normal(key, extent, jnp.float32) * spread * level
    return jnp.minimum(jnp.maximum(values, -limit), limit).astype(kind)


def setup_inputs(seed: int = 0) -> dict:
    key_of = jax.random.split(jax.random.key(seed), 10)
    return {
        "tokens": gaussian(key_of[0], (REPLICA_COUNT, TOK, MODEL_WIDTH), 1.0, 6.0, ((0, 16), (1, 8))),
        "norm_gain": jnp.clip(1.0 + 0.1 * jax.random.normal(key_of[1], (REPLICA_COUNT, MODEL_WIDTH), jnp.float32), 0.5, 1.5),
        "w_query": gaussian(key_of[2], (REPLICA_COUNT, MODEL_WIDTH, HQ), 1.0, 6.0, ((0, 16), (2, 8))),
        "key_weight": gaussian(key_of[3], (REPLICA_COUNT, MODEL_WIDTH, KEY_FEATURES), 1.0, 6.0, ((0, 16), (2, 8))),
        "value_weight": gaussian(key_of[4], (REPLICA_COUNT, MODEL_WIDTH, KEY_FEATURES), 1.0, 6.0, ((0, 16), (2, 8))),
        "w_out": gaussian(key_of[5], (REPLICA_COUNT, HQ, MODEL_WIDTH), 1.0, 6.0, ((0, 16), (1, 8))),
        "doc_ids": jax.vmap(lambda own: jnp.searchsorted(jnp.cumsum(ragged(own, 4, TOK, TOK // 2, 0)), jnp.arange(TOK), side="right"))(jax.random.split(key_of[6], REPLICA_COUNT)).reshape((REPLICA_COUNT, TOK)).astype(jnp.int32),
        "upstream": gaussian(key_of[7], (REPLICA_COUNT, TOK, MODEL_WIDTH), 1.0, 6.0, ((0, 16), (1, 8))),
        "step_count": jax.random.randint(key_of[8], (1,), 0, 1000).astype(jnp.int32),
    }


eps = 1e-05
weight_rate = 1.0
gain_rate = 0.01

def normalize(inputs, scales):
    values = inputs.astype(jnp.float32)
    mixing_factor = lax.rsqrt(lax.optimization_barrier(jnp.mean(values * values, axis=-1, keepdims=True)) + eps)
    return values * mixing_factor * scales

def visibility(documents):
    places = jnp.arange(documents.shape[0])
    return (documents[:, None] == documents[None, :]) & (places[:, None] >= places[None, :])

def attend(queries, keys, values_in, visible):
    length, kv_count, width = keys.shape
    groups = queries.shape[1] // kv_count
    grouped = queries.reshape(length, kv_count, groups, width)
    scores = jnp.einsum('tkgd,skd->kgts', grouped, keys, preferred_element_type=jnp.float32) * width ** (-0.5)
    scores = jnp.where(visible[None, None], scores, -1e+30)
    weights = jnp.exp(scores)
    probs = (weights / lax.optimization_barrier(jnp.sum(weights, axis=-1, keepdims=True))).astype(jnp.bfloat16)
    mixed = jnp.einsum('kgts,skd->tkgd', probs, values_in, preferred_element_type=jnp.float32)
    return mixed.reshape(length, kv_count * groups, width).astype(jnp.bfloat16)

def project_input(inputs, matrix):
    return (jnp.dot(inputs, matrix, preferred_element_type=jnp.float32) * MODEL_WIDTH ** (-0.5)).astype(jnp.bfloat16)

def update(matrix, gradient):
    return (matrix.astype(jnp.float32) - weight_rate * gradient).astype(jnp.bfloat16)

def replica_step(tokens, norm_gain, w_query, key_weight, value_weight, w_out, documents, upstream):
    length = tokens.shape[0]
    normed = normalize(tokens, norm_gain).astype(jnp.bfloat16)
    queries = project_input(normed, w_query).reshape(length, -1, HEAD)
    keys = project_input(normed, key_weight).reshape(length, -1, HEAD)
    values_in = project_input(normed, value_weight).reshape(length, -1, HEAD)
    visible = visibility(documents)
    attended, pullback = jax.vjp(lambda first, second, third: attend(first, second, third, visible), queries, keys, values_in)
    flat = attended.reshape(length, -1)
    out_scale = HQ ** (-0.5)
    grad_out = jnp.einsum('tj,td->jd', flat, upstream, preferred_element_type=jnp.float32) * out_scale
    d_att = (jnp.einsum('td,jd->tj', upstream, w_out, preferred_element_type=jnp.float32) * out_scale).astype(jnp.bfloat16)
    d_query, d_key, d_value = pullback(d_att.reshape(length, -1, HEAD))
    d_query = d_query.reshape(length, -1)
    d_key = d_key.reshape(length, -1)
    d_value = d_value.reshape(length, -1)
    in_scale = MODEL_WIDTH ** (-0.5)
    grad_query = jnp.einsum('td,tj->dj', normed, d_query, preferred_element_type=jnp.float32) * in_scale
    grad_key = jnp.einsum('td,tj->dj', normed, d_key, preferred_element_type=jnp.float32) * in_scale
    grad_value = jnp.einsum('td,tj->dj', normed, d_value, preferred_element_type=jnp.float32) * in_scale
    back = jnp.einsum('tj,dj->td', d_query, w_query, preferred_element_type=jnp.float32)
    back = back + jnp.einsum('tj,dj->td', d_key, key_weight, preferred_element_type=jnp.float32)
    back = back + jnp.einsum('tj,dj->td', d_value, value_weight, preferred_element_type=jnp.float32)
    d_normed = (back * in_scale).astype(jnp.bfloat16)
    unused, norm_pull = jax.vjp(normalize, tokens, norm_gain)
    input_grad, gain_gradient = norm_pull(d_normed.astype(jnp.float32))
    return (update(w_query, grad_query), update(key_weight, grad_key), update(value_weight, grad_value), update(w_out, grad_out), norm_gain - gain_rate * gain_gradient, input_grad)

def reference(tokens, norm_gain, w_query, key_weight, value_weight, w_out, doc_ids, upstream, step_count):
    stepped = lax.map(lambda items: replica_step(*items), (tokens, norm_gain, w_query, key_weight, value_weight, w_out, doc_ids, upstream))
    rounds = N_DP.bit_length() - 1
    distance = jnp.left_shift(jnp.int32(1), (step_count[0] % rounds).astype(jnp.int32))

    def average(array):
        total = array.astype(jnp.float32) + jnp.roll(array, distance, axis=0).astype(jnp.float32)
        return (total * 0.5).astype(array.dtype)
    return (average(stepped[0]), average(stepped[1]), average(stepped[2]), average(stepped[3]), average(stepped[4]), stepped[5])
```

```python
import functools

import jax
import jax.numpy as jnp
from jax import lax
from jax.sharding import PartitionSpec as P

MODEL_WIDTH = 4096
HEAD = 128
HQ = 4096

eps = 1e-05
weight_rate = 1.0
gain_rate = 0.01

X, Y, Z = 4, 4, 4
PLACES = ((0, 0), (0, 1), (1, 0), (1, 1), (3, 0), (3, 1), (2, 0), (2, 1))


def device(x, y, z, core):
    return ((z % 2 * X + x) * 2 + core) * 2 * Y + y * 2 + z // 2


def move(array, dx, dy, dz):
    pairs = [
        (device(x, y, z, core), device((x + dx) % X, (y + dy) % Y, (z + dz) % Z, core))
        for x in range(X)
        for y in range(Y)
        for z in range(Z)
        for core in range(2)
    ]
    return lax.ppermute(array, ("dp", "tensor"), pairs)


def across(array, dx, dy):
    half = array.shape[0] // 2
    up = move(array[:half], dx, dy, 1)
    down = move(array[half:], -dx, -dy, -1)
    up = move(up, -dx, -dy, 1)
    down = move(down, dx, dy, -1)
    return jnp.concatenate([up, down], axis=0)


def from_place(array, dy, dz):
    pairs = [
        (((y + dy) % Y) * 2 + (z ^ dz), y * 2 + z) for y in range(Y) for z in range(2)
    ]
    return lax.ppermute(array, "tensor", pairs)


def to_place(array, dy, dz):
    return from_place(array, (Y - dy) % Y, dz)


def crossed(array, dy, dz):
    pairs = [(y * 2 + z, (y ^ dy) * 2 + (z ^ dz)) for y in range(Y) for z in range(2)]
    return lax.ppermute(array, "tensor", pairs)


def sum_all(array):
    for dy, dz in ((1, 1), (2, 0), (1, 0)):
        array = array + crossed(array, dy, dz)
    return array


def from_behind(array, by):
    count = lax.axis_size("dp")
    return lax.ppermute(array, "dp", [(i, (i + by) % count) for i in range(count)])


def after(array, *others):
    return lax.optimization_barrier((array,) + others)[0]


def gather_first(own, opened, *later):
    beside = [from_place(own, dy, 0) for dy in (1, 3)]
    opened = after(opened, *later)
    return beside + [from_place(opened, dy, 0) for dy in (1, 3)]


def gather_second(own, opened, parts):
    s10, s30, s11, s31 = parts
    s20 = from_place(s10, 1, 0)
    s21 = from_place(s31, 3, 0)
    return jnp.concatenate([own, opened, s10, s11, s30, s31, s20, s21], axis=0)


def scatter_first(rows, count):
    pair = 2 * count
    return [
        to_place(rows[i * pair:(i + 1) * pair], dy, 0) for i, dy in enumerate((0, 1, 3, 2)) if dy
    ]


def scatter_second(rows, count, parts, detour):
    total = rows[:2 * count].astype(jnp.float32)
    for part in parts:
        total = total + part.astype(jnp.float32)
    other = across(total[count:].astype(rows.dtype), *detour)
    return total[:count] + other.astype(jnp.float32)


def normalize(inputs, scales):
    values = inputs.astype(jnp.float32)
    mixing_factor = lax.rsqrt(jnp.mean(values * values, axis=-1, keepdims=True) + eps)
    return values * mixing_factor * scales


def attend(queries, keys, values_in, visible):
    length, kv_count, width = keys.shape
    groups = queries.shape[1] // kv_count
    grouped = queries.reshape(length, kv_count, groups, width)
    scores = jnp.einsum(
        "tkgd,skd->kgts", grouped, keys, preferred_element_type=jnp.float32
    ) * width ** (-0.5)
    scores = jnp.where(visible[None, None], scores, -1e30)
    weights = jnp.exp(scores)
    probs = (weights / jnp.sum(weights, axis=-1, keepdims=True)).astype(jnp.bfloat16)
    mixed = jnp.einsum("kgts,skd->tkgd", probs, values_in, preferred_element_type=jnp.float32)
    return mixed.reshape(length, kv_count * groups, width).astype(jnp.bfloat16)


def project_input(inputs, matrix):
    return (
        jnp.dot(inputs, matrix, preferred_element_type=jnp.float32) * MODEL_WIDTH ** (-0.5)
    ).astype(jnp.bfloat16)


def update(matrix, gradient):
    return (matrix.astype(jnp.float32) - weight_rate * gradient).astype(jnp.bfloat16)


def average(mine, other):
    return ((mine.astype(jnp.float32) + other.astype(jnp.float32)) * 0.5).astype(mine.dtype)


def step(
    distance, own_rows, gain_vec, query_mat, key_mat, value_mat, out_mat, documents, own_upstream
):
    detour = (1, 0) if distance == 8 else (0, 1)
    count = own_rows.shape[0]
    out_scale = HQ ** (-0.5)
    in_scale = MODEL_WIDTH ** (-0.5)

    index = lax.axis_index("tensor")
    place = jnp.stack([((index // 2 + dy) % Y) * 2 + ((index % 2) ^ dz) for dy, dz in PLACES])
    chosen = (place[:, None] == jnp.arange(len(PLACES))[None, :]).astype(jnp.int32)
    documents = jnp.sum(
        chosen[:, :, None] * documents.reshape(1, len(PLACES), count), axis=1
    ).reshape(-1)
    places = (place[:, None] * count + jnp.arange(count)[None, :]).reshape(-1)
    visible = (documents[:, None] == documents[None, :]) & (places[:, None] >= places[None, :])

    own_normed, norm_pull = jax.vjp(normalize, own_rows, gain_vec)
    own_normed = own_normed.astype(jnp.bfloat16)
    half = out_mat.shape[0] // 2
    peer_mat = [from_behind(out_mat[i:i + half], distance) for i in (0, half)]
    peer_rows = from_behind(own_upstream, distance)

    opened_normed = across(own_normed, *detour)
    normed_parts = gather_first(own_normed, opened_normed)
    normed = gather_second(own_normed, opened_normed, normed_parts)
    own_upstream = after(own_upstream, *normed_parts)
    opened_upstream = across(own_upstream, *detour)
    upstream_parts = gather_first(own_upstream, opened_upstream, peer_mat[0])
    upstream_parts = lax.optimization_barrier((*upstream_parts, normed))[:-1]
    upstream = gather_second(own_upstream, opened_upstream, upstream_parts)

    length = normed.shape[0]
    queries = project_input(normed, query_mat).reshape(length, -1, HEAD)
    keys = project_input(normed, key_mat).reshape(length, -1, HEAD)
    values_in = project_input(normed, value_mat).reshape(length, -1, HEAD)
    attended, pullback = jax.vjp(
        lambda first, second, third: attend(first, second, third, visible), queries, keys, values_in
    )
    flat = attended.reshape(length, -1)
    peer_flat = from_behind(flat, distance)
    part = (
        jnp.einsum("td,jd->tj", upstream, out_mat, preferred_element_type=jnp.float32) * out_scale
    ).astype(jnp.bfloat16)
    d_query, d_key, d_value = pullback(part.reshape(length, -1, HEAD))
    d_query, d_key, d_value = lax.optimization_barrier((d_query, d_key, d_value, peer_mat[1]))[:3]
    d_query = d_query.reshape(length, -1)
    d_key = d_key.reshape(length, -1)
    d_value = d_value.reshape(length, -1)

    def grown(matrix, rows, gradient):
        return update(
            matrix,
            jnp.einsum("td,tj->dj", rows, gradient, preferred_element_type=jnp.float32)
            * in_scale,
        )

    new_query = grown(query_mat, normed, d_query)
    peer_query = from_behind(new_query, distance)
    new_key = grown(key_mat, normed, d_key)
    peer_key = from_behind(new_key, distance)
    new_value = grown(value_mat, normed, d_value)
    peer_value = from_behind(after(new_value, peer_query), distance)

    total = jnp.einsum("tj,dj->td", d_query, query_mat, preferred_element_type=jnp.float32)
    total = total + jnp.einsum("tj,dj->td", d_key, key_mat, preferred_element_type=jnp.float32)
    total = total + jnp.einsum("tj,dj->td", d_value, value_mat, preferred_element_type=jnp.float32)
    total = (total * in_scale).astype(jnp.bfloat16)
    scattered = scatter_first(after(total, peer_rows, peer_flat), count)
    d_normed = scatter_second(total, count, scattered, detour).astype(jnp.bfloat16)
    input_grad, gain_part = norm_pull(d_normed.astype(jnp.float32))
    new_gain = gain_vec - gain_rate * sum_all(gain_part)
    peer_gain = from_behind(new_gain, distance)

    peer_rows = after(peer_rows, d_normed)
    opened_peer = across(peer_rows, *detour)
    peer_parts = gather_first(peer_rows, opened_peer)
    peer_parts = lax.optimization_barrier((*peer_parts, peer_query))[:-1]
    peer_upstream = gather_second(peer_rows, opened_peer, peer_parts)
    peer_upstream = after(peer_upstream, peer_key)

    def grown_out(matrix, flat, rows):
        return update(
            matrix,
            jnp.einsum("tj,td->jd", flat, rows, preferred_element_type=jnp.float32) * out_scale,
        )

    new_out = grown_out(out_mat, flat, upstream)
    peer_out = grown_out(jnp.concatenate(peer_mat, axis=0), peer_flat, peer_upstream)
    return (
        average(new_query, after(peer_query, peer_value))[None],
        average(new_key, after(peer_key, peer_upstream))[None],
        average(new_value, peer_value)[None],
        average(new_out, peer_out)[None],
        average(new_gain, after(peer_gain, peer_value))[None],
        input_grad[None],
    )


def per_device(
    tokens, norm_gain, w_query, key_weight, value_weight, w_out, doc_ids, upstream, step_count
):
    rounds = lax.axis_size("dp").bit_length() - 1
    which = step_count[0] % rounds
    return lax.switch(
        which,
        [functools.partial(step, 2**level) for level in range(rounds)],
        tokens[0],
        norm_gain[0],
        w_query[0],
        key_weight[0],
        value_weight[0],
        w_out[0],
        doc_ids[0],
        upstream[0],
    )


def solution(mesh):
    return jax.shard_map(
        per_device,
        mesh=mesh,
        in_specs=(
            P("dp", "tensor", None),
            P("dp", None),
            P("dp", None, "tensor"),
            P("dp", None, "tensor"),
            P("dp", None, "tensor"),
            P("dp", "tensor", None),
            P("dp", None),
            P("dp", "tensor", None),
            P(),
        ),
        out_specs=(
            P("dp", None, "tensor"),
            P("dp", None, "tensor"),
            P("dp", None, "tensor"),
            P("dp", "tensor", None),
            P("dp", None),
            P("dp", "tensor", None),
        ),
        check_vma=False,
    )
```

```python
import functools

import jax
import jax.numpy as jnp
from jax import lax
from jax.sharding import PartitionSpec as P

MODEL_WIDTH = 4096
HEAD = 128
HQ = 4096

eps = 1e-05
weight_rate = 1.0
gain_rate = 0.01

X, Y, Z = 4, 4, 4
PLACES = ((0, 0), (0, 1), (1, 0), (1, 1), (3, 0), (3, 1), (2, 0), (2, 1))


def device(x, y, z, core):
    return ((z % 2 * X + x) * 2 + core) * 2 * Y + y * 2 + z // 2


def move(array, dx, dy, dz):
    pairs = [
        (device(x, y, z, core), device((x + dx) % X, (y + dy) % Y, (z + dz) % Z, core))
        for x in range(X)
        for y in range(Y)
        for z in range(Z)
        for core in range(2)
    ]
    return lax.ppermute(array, ("dp", "tensor"), pairs)


def across(array, dx, dy):
    half = array.shape[0] // 2
    up = move(array[:half], dx, dy, 1)
    down = move(array[half:], -dx, -dy, -1)
    up = move(up, -dx, -dy, 1)
    down = move(down, dx, dy, -1)
    return jnp.concatenate([up, down], axis=0)


def from_place(array, dy, dz):
    pairs = [
        (((y + dy) % Y) * 2 + (z ^ dz), y * 2 + z) for y in range(Y) for z in range(2)
    ]
    return lax.ppermute(array, "tensor", pairs)


def to_place(array, dy, dz):
    return from_place(array, (Y - dy) % Y, dz)


def crossed(array, dy, dz):
    pairs = [(y * 2 + z, (y ^ dy) * 2 + (z ^ dz)) for y in range(Y) for z in range(2)]
    return lax.ppermute(array, "tensor", pairs)


def sum_all(array):
    for dy, dz in ((1, 1), (2, 0), (1, 0)):
        array = array + crossed(array, dy, dz)
    return array


def from_behind(array, by):
    count = lax.axis_size("dp")
    return lax.ppermute(array, "dp", [(i, (i + by) % count) for i in range(count)])


def after(array, *others):
    return lax.optimization_barrier((array,) + others)[0]


def gather_first(own, opened, *later):
    beside = [from_place(own, dy, 0) for dy in (1, 3)]
    opened = after(opened, *later)
    return beside + [from_place(opened, dy, 0) for dy in (1, 3)]


def gather_second(own, opened, parts):
    s10, s30, s11, s31 = parts
    s20 = from_place(s10, 1, 0)
    s21 = from_place(s31, 3, 0)
    return jnp.concatenate([own, opened, s10, s11, s30, s31, s20, s21], axis=0)


def scatter_first(rows, count):
    pair = 2 * count
    return [
        to_place(rows[i * pair:(i + 1) * pair], dy, 0) for i, dy in enumerate((0, 1, 3, 2)) if dy
    ]


def scatter_second(rows, count, parts, detour):
    total = rows[:2 * count].astype(jnp.float32)
    for part in parts:
        total = total + part.astype(jnp.float32)
    other = across(total[count:].astype(rows.dtype), *detour)
    return total[:count] + other.astype(jnp.float32)


def normalize(inputs, scales):
    values = inputs.astype(jnp.float32)
    mixing_factor = lax.rsqrt(jnp.mean(values * values, axis=-1, keepdims=True) + eps)
    return values * mixing_factor * scales


def attend(queries, keys, values_in, visible):
    length, kv_count, width = keys.shape
    groups = queries.shape[1] // kv_count
    grouped = queries.reshape(length, kv_count, groups, width)
    scores = jnp.einsum(
        "tkgd,skd->kgts", grouped, keys, preferred_element_type=jnp.float32
    ) * width ** (-0.5)
    scores = jnp.where(visible[None, None], scores, -1e30)
    weights = jnp.exp(scores)
    probs = (weights / jnp.sum(weights, axis=-1, keepdims=True)).astype(jnp.bfloat16)
    mixed = jnp.einsum("kgts,skd->tkgd", probs, values_in, preferred_element_type=jnp.float32)
    return mixed.reshape(length, kv_count * groups, width).astype(jnp.bfloat16)


def project_input(inputs, matrix):
    return (
        jnp.dot(inputs, matrix, preferred_element_type=jnp.float32) * MODEL_WIDTH ** (-0.5)
    ).astype(jnp.bfloat16)


def update(matrix, gradient):
    return (matrix.astype(jnp.float32) - weight_rate * gradient).astype(jnp.bfloat16)


def average(mine, other):
    return ((mine.astype(jnp.float32) + other.astype(jnp.float32)) * 0.5).astype(mine.dtype)


def step(
    distance, own_rows, gain_vec, query_mat, key_mat, value_mat, out_mat, documents, own_upstream
):
    detour = (1, 0) if distance == 8 else (0, 1)
    count = own_rows.shape[0]
    out_scale = HQ ** (-0.5)
    in_scale = MODEL_WIDTH ** (-0.5)

    index = lax.axis_index("tensor")
    place = jnp.stack([((index // 2 + dy) % Y) * 2 + ((index % 2) ^ dz) for dy, dz in PLACES])
    chosen = (place[:, None] == jnp.arange(len(PLACES))[None, :]).astype(jnp.int32)
    documents = jnp.sum(
        chosen[:, :, None] * documents.reshape(1, len(PLACES), count), axis=1
    ).reshape(-1)
    places = (place[:, None] * count + jnp.arange(count)[None, :]).reshape(-1)
    visible = (documents[:, None] == documents[None, :]) & (places[:, None] >= places[None, :])

    own_normed, norm_pull = jax.vjp(normalize, own_rows, gain_vec)
    own_normed = own_normed.astype(jnp.bfloat16)
    half = out_mat.shape[0] // 2
    peer_mat = [from_behind(out_mat[i:i + half], distance) for i in (0, half)]
    peer_rows = from_behind(own_upstream, distance)

    opened_normed = across(own_normed, *detour)
    normed_parts = gather_first(own_normed, opened_normed)
    normed = gather_second(own_normed, opened_normed, normed_parts)
    own_upstream = after(own_upstream, *normed_parts)
    opened_upstream = across(own_upstream, *detour)
    upstream_parts = gather_first(own_upstream, opened_upstream, peer_mat[0])
    upstream_parts = lax.optimization_barrier((*upstream_parts, normed))[:-1]
    upstream = gather_second(own_upstream, opened_upstream, upstream_parts)

    length = normed.shape[0]
    queries = project_input(normed, query_mat).reshape(length, -1, HEAD)
    keys = project_input(normed, key_mat).reshape(length, -1, HEAD)
    values_in = project_input(normed, value_mat).reshape(length, -1, HEAD)
    attended, pullback = jax.vjp(
        lambda first, second, third: attend(first, second, third, visible), queries, keys, values_in
    )
    flat = attended.reshape(length, -1)
    peer_flat = from_behind(flat, distance)
    part = (
        jnp.einsum("td,jd->tj", upstream, out_mat, preferred_element_type=jnp.float32) * out_scale
    ).astype(jnp.bfloat16)
    d_query, d_key, d_value = pullback(part.reshape(length, -1, HEAD))
    d_query, d_key, d_value = lax.optimization_barrier((d_query, d_key, d_value, peer_mat[1]))[:3]
    d_query = d_query.reshape(length, -1)
    d_key = d_key.reshape(length, -1)
    d_value = d_value.reshape(length, -1)

    def grown(matrix, rows, gradient):
        return update(
            matrix,
            jnp.einsum("td,tj->dj", rows, gradient, preferred_element_type=jnp.float32)
            * in_scale,
        )

    new_query = grown(query_mat, normed, d_query)
    peer_query = from_behind(new_query, distance)
    new_key = grown(key_mat, normed, d_key)
    peer_key = from_behind(new_key, distance)
    new_value = grown(value_mat, normed, d_value)
    peer_value = from_behind(after(new_value, peer_query), distance)

    total = jnp.einsum("tj,dj->td", d_query, query_mat, preferred_element_type=jnp.float32)
    total = total + jnp.einsum("tj,dj->td", d_key, key_mat, preferred_element_type=jnp.float32)
    total = total + jnp.einsum("tj,dj->td", d_value, value_mat, preferred_element_type=jnp.float32)
    total = (total * in_scale).astype(jnp.bfloat16)
    scattered = scatter_first(after(total, peer_rows, peer_flat), count)
    d_normed = scatter_second(total, count, scattered, detour).astype(jnp.bfloat16)
    input_grad, gain_part = norm_pull(d_normed.astype(jnp.float32))
    new_gain = gain_vec - gain_rate * sum_all(gain_part)
    peer_gain = from_behind(new_gain, distance)

    peer_rows = after(peer_rows, d_normed)
    opened_peer = across(peer_rows, *detour)
    peer_parts = gather_first(peer_rows, opened_peer)
    peer_parts = lax.optimization_barrier((*peer_parts, peer_query))[:-1]
    peer_upstream = gather_second(peer_rows, opened_peer, peer_parts)
    peer_upstream = after(peer_upstream, peer_key)

    def grown_out(matrix, flat, rows):
        return update(
            matrix,
            jnp.einsum("tj,td->jd", flat, rows, preferred_element_type=jnp.float32) * out_scale,
        )

    new_out = grown_out(out_mat, flat, upstream)
    peer_out = grown_out(jnp.concatenate(peer_mat, axis=0), peer_flat, peer_upstream)
    return (
        average(new_query, after(peer_query, peer_value))[None],
        average(new_key, after(peer_key, peer_upstream))[None],
        average(new_value, peer_value)[None],
        average(new_out, peer_out)[None],
        average(new_gain, after(peer_gain, peer_value))[None],
        input_grad[None],
    )


def per_device(
    tokens, norm_gain, w_query, key_weight, value_weight, w_out, doc_ids, upstream, step_count
):
    rounds = lax.axis_size("dp").bit_length() - 1
    which = step_count[0] % rounds
    items = (
        tokens[0],
        norm_gain[0],
        w_query[0],
        key_weight[0],
        value_weight[0],
        w_out[0],
        doc_ids[0],
        upstream[0],
    )

    def choose(low, high, items):
        if high - low == 1:
            return step(2**low, *items)
        middle = (low + high) // 2
        return lax.cond(
            which < middle,
            functools.partial(choose, low, middle),
            functools.partial(choose, middle, high),
            items,
        )

    return choose(0, rounds, items)


def solution(mesh):
    return jax.shard_map(
        per_device,
        mesh=mesh,
        in_specs=(
            P("dp", "tensor", None),
            P("dp", None),
            P("dp", None, "tensor"),
            P("dp", None, "tensor"),
            P("dp", None, "tensor"),
            P("dp", "tensor", None),
            P("dp", None),
            P("dp", "tensor", None),
            P(),
        ),
        out_specs=(
            P("dp", None, "tensor"),
            P("dp", None, "tensor"),
            P("dp", None, "tensor"),
            P("dp", "tensor", None),
            P("dp", None),
            P("dp", "tensor", None),
        ),
        check_vma=False,
    )
```

```python
import functools

import jax
import jax.numpy as jnp
from jax import lax
from jax.sharding import PartitionSpec as P

MODEL_WIDTH = 4096
HEAD = 128
HQ = 4096

eps = 1e-05
weight_rate = 1.0
gain_rate = 0.01

X, Y, Z = 4, 4, 4
PLACES = ((0, 0), (0, 1), (1, 0), (1, 1), (3, 0), (3, 1), (2, 0), (2, 1))


def device(x, y, z, core):
    return ((z % 2 * X + x) * 2 + core) * 2 * Y + y * 2 + z // 2


def move(array, dx, dy, dz):
    pairs = [
        (device(x, y, z, core), device((x + dx) % X, (y + dy) % Y, (z + dz) % Z, core))
        for x in range(X)
        for y in range(Y)
        for z in range(Z)
        for core in range(2)
    ]
    return lax.ppermute(array, ("dp", "tensor"), pairs)


def across(array, dx, dy):
    half = array.shape[0] // 2
    up = move(array[:half], dx, dy, 1)
    down = move(array[half:], -dx, -dy, -1)
    up = move(up, -dx, -dy, 1)
    down = move(down, dx, dy, -1)
    return jnp.concatenate([up, down], axis=0)


def from_place(array, dy, dz):
    pairs = [
        (((y + dy) % Y) * 2 + (z ^ dz), y * 2 + z) for y in range(Y) for z in range(2)
    ]
    return lax.ppermute(array, "tensor", pairs)


def to_place(array, dy, dz):
    return from_place(array, (Y - dy) % Y, dz)


def crossed(array, dy, dz):
    pairs = [(y * 2 + z, (y ^ dy) * 2 + (z ^ dz)) for y in range(Y) for z in range(2)]
    return lax.ppermute(array, "tensor", pairs)


def sum_all(array):
    for dy, dz in ((1, 1), (2, 0), (1, 0)):
        array = array + crossed(array, dy, dz)
    return array


def from_behind(array, by):
    count = lax.axis_size("dp")
    return lax.ppermute(array, "dp", [(i, (i + by) % count) for i in range(count)])


def after(array, *others):
    return lax.optimization_barrier((array,) + others)[0]


def gather_first(own, opened, *later):
    beside = [from_place(own, dy, 0) for dy in (1, 3)]
    opened = after(opened, *later)
    return beside + [from_place(opened, dy, 0) for dy in (1, 3)]


def gather_second(own, opened, parts):
    s10, s30, s11, s31 = parts
    s20 = from_place(s10, 1, 0)
    s21 = from_place(s31, 3, 0)
    return jnp.concatenate([own, opened, s10, s11, s30, s31, s20, s21], axis=0)


def scatter_first(rows, count):
    pair = 2 * count
    return [
        to_place(rows[i * pair:(i + 1) * pair], dy, 0) for i, dy in enumerate((0, 1, 3, 2)) if dy
    ]


def scatter_second(rows, count, parts, detour):
    total = rows[:2 * count].astype(jnp.float32)
    for part in parts:
        total = total + part.astype(jnp.float32)
    other = across(total[count:].astype(rows.dtype), *detour)
    return total[:count] + other.astype(jnp.float32)


def normalize(inputs, scales):
    values = inputs.astype(jnp.float32)
    mixing_factor = lax.rsqrt(jnp.mean(values * values, axis=-1, keepdims=True) + eps)
    return values * mixing_factor * scales


def attend(queries, keys, values_in, visible):
    length, kv_count, width = keys.shape
    groups = queries.shape[1] // kv_count
    grouped = queries.reshape(length, kv_count, groups, width)
    scores = jnp.einsum(
        "tkgd,skd->kgts", grouped, keys, preferred_element_type=jnp.float32
    ) * width ** (-0.5)
    scores = jnp.where(visible[None, None], scores, -1e30)
    weights = jnp.exp(scores)
    probs = (weights / jnp.sum(weights, axis=-1, keepdims=True)).astype(jnp.bfloat16)
    mixed = jnp.einsum("kgts,skd->tkgd", probs, values_in, preferred_element_type=jnp.float32)
    return mixed.reshape(length, kv_count * groups, width).astype(jnp.bfloat16)


def project_input(inputs, matrix):
    return (
        jnp.dot(inputs, matrix, preferred_element_type=jnp.float32) * MODEL_WIDTH ** (-0.5)
    ).astype(jnp.bfloat16)


def update(matrix, gradient):
    return (matrix.astype(jnp.float32) - weight_rate * gradient).astype(jnp.bfloat16)


def average(mine, other):
    return ((mine.astype(jnp.float32) + other.astype(jnp.float32)) * 0.5).astype(mine.dtype)


def step(
    distance, own_rows, gain_vec, query_mat, key_mat, value_mat, out_mat, documents, own_upstream
):
    detour = (1, 0) if distance == 8 else (0, 1)
    count = own_rows.shape[0]
    out_scale = HQ ** (-0.5)
    in_scale = MODEL_WIDTH ** (-0.5)

    index = lax.axis_index("tensor")
    place = jnp.stack([((index // 2 + dy) % Y) * 2 + ((index % 2) ^ dz) for dy, dz in PLACES])
    chosen = (place[:, None] == jnp.arange(len(PLACES))[None, :]).astype(jnp.int32)
    documents = jnp.sum(
        chosen[:, :, None] * documents.reshape(1, len(PLACES), count), axis=1
    ).reshape(-1)
    places = (place[:, None] * count + jnp.arange(count)[None, :]).reshape(-1)
    visible = (documents[:, None] == documents[None, :]) & (places[:, None] >= places[None, :])

    own_normed, norm_pull = jax.vjp(normalize, own_rows, gain_vec)
    own_normed = own_normed.astype(jnp.bfloat16)
    peer_mat = from_behind(out_mat, distance)

    opened_normed = across(own_normed, *detour)
    normed_parts = gather_first(own_normed, opened_normed)
    normed = gather_second(own_normed, opened_normed, normed_parts)
    own_upstream = after(own_upstream, *normed_parts)
    opened_upstream = across(own_upstream, *detour)
    upstream_parts = gather_first(own_upstream, opened_upstream)
    upstream_parts = lax.optimization_barrier((*upstream_parts, normed))[:-1]
    peer_rows = from_behind(after(own_upstream, *upstream_parts), distance)
    upstream = gather_second(own_upstream, opened_upstream, upstream_parts)

    length = normed.shape[0]
    queries = project_input(normed, query_mat).reshape(length, -1, HEAD)
    keys = project_input(normed, key_mat).reshape(length, -1, HEAD)
    values_in = project_input(normed, value_mat).reshape(length, -1, HEAD)
    attended, pullback = jax.vjp(
        lambda first, second, third: attend(first, second, third, visible), queries, keys, values_in
    )
    flat = attended.reshape(length, -1)
    peer_flat = from_behind(flat, distance)
    upstream = after(upstream, peer_mat)
    part = (
        jnp.einsum("td,jd->tj", upstream, out_mat, preferred_element_type=jnp.float32) * out_scale
    ).astype(jnp.bfloat16)
    d_query, d_key, d_value = pullback(part.reshape(length, -1, HEAD))
    d_query = d_query.reshape(length, -1)
    d_key = d_key.reshape(length, -1)
    d_value = d_value.reshape(length, -1)

    def grown(matrix, rows, gradient):
        return update(
            matrix,
            jnp.einsum("td,tj->dj", rows, gradient, preferred_element_type=jnp.float32)
            * in_scale,
        )

    new_query = grown(query_mat, normed, d_query)
    peer_query = from_behind(new_query, distance)
    new_key = grown(key_mat, normed, d_key)
    peer_key = from_behind(new_key, distance)
    new_value = grown(value_mat, normed, d_value)
    peer_value = from_behind(after(new_value, peer_query), distance)

    d_query, d_key, d_value = lax.optimization_barrier((d_query, d_key, d_value, new_query))[:3]
    total = jnp.einsum("tj,dj->td", d_query, query_mat, preferred_element_type=jnp.float32)
    total = total + jnp.einsum("tj,dj->td", d_key, key_mat, preferred_element_type=jnp.float32)
    total = total + jnp.einsum("tj,dj->td", d_value, value_mat, preferred_element_type=jnp.float32)
    total = (total * in_scale).astype(jnp.bfloat16)
    scattered = scatter_first(after(total, peer_rows, peer_flat), count)
    d_normed = scatter_second(total, count, scattered, detour).astype(jnp.bfloat16)
    input_grad, gain_part = norm_pull(d_normed.astype(jnp.float32))
    new_gain = gain_vec - gain_rate * sum_all(gain_part)
    peer_gain = from_behind(new_gain, distance)

    peer_rows = after(peer_rows, d_normed)
    opened_peer = across(peer_rows, *detour)
    peer_parts = gather_first(peer_rows, opened_peer)
    peer_parts = lax.optimization_barrier((*peer_parts, peer_query, peer_key))[:-2]
    peer_upstream = gather_second(peer_rows, opened_peer, peer_parts)

    def grown_out(matrix, flat, rows):
        return update(
            matrix,
            jnp.einsum("tj,td->jd", flat, rows, preferred_element_type=jnp.float32) * out_scale,
        )

    new_out = grown_out(out_mat, flat, upstream)
    peer_out = grown_out(peer_mat, peer_flat, peer_upstream)
    return (
        average(new_query, after(peer_query, peer_value))[None],
        average(new_key, after(peer_key, peer_upstream))[None],
        average(new_value, peer_value)[None],
        average(new_out, peer_out)[None],
        average(new_gain, after(peer_gain, peer_value))[None],
        input_grad[None],
    )


def per_device(
    tokens, norm_gain, w_query, key_weight, value_weight, w_out, doc_ids, upstream, step_count
):
    rounds = lax.axis_size("dp").bit_length() - 1
    which = step_count[0] % rounds
    items = (
        tokens[0],
        norm_gain[0],
        w_query[0],
        key_weight[0],
        value_weight[0],
        w_out[0],
        doc_ids[0],
        upstream[0],
    )

    def choose(low, high, items):
        if high - low == 1:
            return step(2**low, *items)
        middle = (low + high) // 2
        return lax.cond(
            which < middle,
            functools.partial(choose, low, middle),
            functools.partial(choose, middle, high),
            items,
        )

    return choose(0, rounds, items)


def solution(mesh):
    return jax.shard_map(
        per_device,
        mesh=mesh,
        in_specs=(
            P("dp", "tensor", None),
            P("dp", None),
            P("dp", None, "tensor"),
            P("dp", None, "tensor"),
            P("dp", None, "tensor"),
            P("dp", "tensor", None),
            P("dp", None),
            P("dp", "tensor", None),
            P(),
        ),
        out_specs=(
            P("dp", None, "tensor"),
            P("dp", None, "tensor"),
            P("dp", None, "tensor"),
            P("dp", "tensor", None),
            P("dp", None),
            P("dp", "tensor", None),
        ),
        check_vma=False,
    )
```

```python
import functools

import jax
import jax.numpy as jnp
from jax import lax
from jax.sharding import PartitionSpec as P

MODEL_WIDTH = 4096
HEAD = 128
HQ = 4096

eps = 1e-05
weight_rate = 1.0
gain_rate = 0.01

X, Y, Z = 4, 4, 4
PLACES = ((0, 0), (0, 1), (1, 0), (1, 1), (3, 0), (3, 1), (2, 0), (2, 1))


def device(x, y, z, core):
    return ((z % 2 * X + x) * 2 + core) * 2 * Y + y * 2 + z // 2


def move(array, dx, dy, dz):
    pairs = [
        (device(x, y, z, core), device((x + dx) % X, (y + dy) % Y, (z + dz) % Z, core))
        for x in range(X)
        for y in range(Y)
        for z in range(Z)
        for core in range(2)
    ]
    return lax.ppermute(array, ("dp", "tensor"), pairs)


def across(array, dx, dy):
    half = array.shape[0] // 2
    up = move(array[:half], dx, dy, 1)
    down = move(array[half:], -dx, -dy, -1)
    up = move(up, -dx, -dy, 1)
    down = move(down, dx, dy, -1)
    return jnp.concatenate([up, down], axis=0)


def from_place(array, dy, dz):
    pairs = [
        (((y + dy) % Y) * 2 + (z ^ dz), y * 2 + z) for y in range(Y) for z in range(2)
    ]
    return lax.ppermute(array, "tensor", pairs)


def to_place(array, dy, dz):
    return from_place(array, (Y - dy) % Y, dz)


def crossed(array, dy, dz):
    pairs = [(y * 2 + z, (y ^ dy) * 2 + (z ^ dz)) for y in range(Y) for z in range(2)]
    return lax.ppermute(array, "tensor", pairs)


def sum_all(array):
    for dy, dz in ((1, 1), (2, 0), (1, 0)):
        array = array + crossed(array, dy, dz)
    return array


def from_behind(array, by):
    count = lax.axis_size("dp")
    return lax.ppermute(array, "dp", [(i, (i + by) % count) for i in range(count)])


def after(array, *others):
    return lax.optimization_barrier((array,) + others)[0]


def gather_first(own, opened, *later):
    beside = [from_place(own, dy, 0) for dy in (1, 3)]
    opened = after(opened, *later)
    return beside + [from_place(opened, dy, 0) for dy in (1, 3)]


def gather_second(own, opened, parts):
    s10, s30, s11, s31 = parts
    s20 = from_place(s10, 1, 0)
    s21 = from_place(s31, 3, 0)
    return jnp.concatenate([own, opened, s10, s11, s30, s31, s20, s21], axis=0)


def scatter_first(rows, count):
    pair = 2 * count
    return [
        to_place(rows[i * pair:(i + 1) * pair], dy, 0) for i, dy in enumerate((0, 1, 3, 2)) if dy
    ]


def scatter_second(rows, count, parts, detour):
    total = rows[:2 * count].astype(jnp.float32)
    for part in parts:
        total = total + part.astype(jnp.float32)
    other = across(total[count:].astype(rows.dtype), *detour)
    return total[:count] + other.astype(jnp.float32)


def normalize(inputs, scales):
    values = inputs.astype(jnp.float32)
    mixing_factor = lax.rsqrt(jnp.mean(values * values, axis=-1, keepdims=True) + eps)
    return values * mixing_factor * scales


def attend(queries, keys, values_in, visible):
    length, kv_count, width = keys.shape
    groups = queries.shape[1] // kv_count
    grouped = queries.reshape(length, kv_count, groups, width)
    scores = jnp.einsum(
        "tkgd,skd->kgts", grouped, keys, preferred_element_type=jnp.float32
    ) * width ** (-0.5)
    scores = jnp.where(visible[None, None], scores, -1e30)
    weights = jnp.exp(scores)
    probs = (weights / jnp.sum(weights, axis=-1, keepdims=True)).astype(jnp.bfloat16)
    mixed = jnp.einsum("kgts,skd->tkgd", probs, values_in, preferred_element_type=jnp.float32)
    return mixed.reshape(length, kv_count * groups, width).astype(jnp.bfloat16)


def project_input(inputs, matrix):
    return (
        jnp.dot(inputs, matrix, preferred_element_type=jnp.float32) * MODEL_WIDTH ** (-0.5)
    ).astype(jnp.bfloat16)


def update(matrix, gradient):
    return (matrix.astype(jnp.float32) - weight_rate * gradient).astype(jnp.bfloat16)


def average(mine, other):
    return ((mine.astype(jnp.float32) + other.astype(jnp.float32)) * 0.5).astype(mine.dtype)


def step(
    distance, own_rows, gain_vec, query_mat, key_mat, value_mat, out_mat, documents, own_upstream
):
    detour = (1, 0) if distance == 8 else (0, 1)
    count = own_rows.shape[0]
    out_scale = HQ ** (-0.5)
    in_scale = MODEL_WIDTH ** (-0.5)

    index = lax.axis_index("tensor")
    place = jnp.stack([((index // 2 + dy) % Y) * 2 + ((index % 2) ^ dz) for dy, dz in PLACES])
    chosen = (place[:, None] == jnp.arange(len(PLACES))[None, :]).astype(jnp.int32)
    documents = jnp.sum(
        chosen[:, :, None] * documents.reshape(1, len(PLACES), count), axis=1
    ).reshape(-1)
    places = (place[:, None] * count + jnp.arange(count)[None, :]).reshape(-1)
    visible = (documents[:, None] == documents[None, :]) & (places[:, None] >= places[None, :])

    own_normed, norm_pull = jax.vjp(normalize, own_rows, gain_vec)
    own_normed = own_normed.astype(jnp.bfloat16)
    half = out_mat.shape[0] // 2
    peer_mat = [from_behind(out_mat[i:i + half], distance) for i in (0, half)]
    peer_rows = from_behind(own_upstream, distance)

    opened_normed = across(own_normed, *detour)
    normed_parts = gather_first(own_normed, opened_normed)
    normed = gather_second(own_normed, opened_normed, normed_parts)
    own_upstream = after(own_upstream, *normed_parts)
    opened_upstream = across(own_upstream, *detour)
    upstream_parts = gather_first(own_upstream, opened_upstream, peer_mat[0])
    upstream_parts = lax.optimization_barrier((*upstream_parts, normed))[:-1]
    upstream = gather_second(own_upstream, opened_upstream, upstream_parts)

    length = normed.shape[0]
    queries = project_input(normed, query_mat).reshape(length, -1, HEAD)
    keys = project_input(normed, key_mat).reshape(length, -1, HEAD)
    values_in = project_input(normed, value_mat).reshape(length, -1, HEAD)
    attended, pullback = jax.vjp(
        lambda first, second, third: attend(first, second, third, visible), queries, keys, values_in
    )
    flat = attended.reshape(length, -1)
    peer_flat = from_behind(flat, distance)
    part = (
        jnp.einsum("td,jd->tj", upstream, out_mat, preferred_element_type=jnp.float32) * out_scale
    ).astype(jnp.bfloat16)
    d_query, d_key, d_value = pullback(part.reshape(length, -1, HEAD))
    d_query, d_key, d_value = lax.optimization_barrier((d_query, d_key, d_value, peer_mat[1]))[:3]
    d_query = d_query.reshape(length, -1)
    d_key = d_key.reshape(length, -1)
    d_value = d_value.reshape(length, -1)

    def grown(matrix, rows, gradient):
        return update(
            matrix,
            jnp.einsum("td,tj->dj", rows, gradient, preferred_element_type=jnp.float32)
            * in_scale,
        )

    new_query = grown(query_mat, normed, d_query)
    peer_query = from_behind(new_query, distance)
    new_key = grown(key_mat, normed, d_key)
    peer_key = from_behind(new_key, distance)
    new_value = grown(value_mat, normed, d_value)
    peer_value = from_behind(after(new_value, peer_query), distance)

    total = jnp.einsum("tj,dj->td", d_query, query_mat, preferred_element_type=jnp.float32)
    total = total + jnp.einsum("tj,dj->td", d_key, key_mat, preferred_element_type=jnp.float32)
    total = total + jnp.einsum("tj,dj->td", d_value, value_mat, preferred_element_type=jnp.float32)
    total = (total * in_scale).astype(jnp.bfloat16)
    scattered = scatter_first(after(total, peer_rows, peer_flat), count)
    d_normed = scatter_second(total, count, scattered, detour).astype(jnp.bfloat16)
    input_grad, gain_part = norm_pull(d_normed.astype(jnp.float32))
    new_gain = gain_vec - gain_rate * sum_all(gain_part)
    peer_gain = from_behind(new_gain, distance)

    peer_rows = after(peer_rows, d_normed)
    opened_peer = across(peer_rows, *detour)
    peer_parts = gather_first(peer_rows, opened_peer)
    peer_parts = lax.optimization_barrier((*peer_parts, peer_query, peer_key))[:-2]
    peer_upstream = gather_second(peer_rows, opened_peer, peer_parts)

    def grown_out(matrix, flat, rows):
        return update(
            matrix,
            jnp.einsum("tj,td->jd", flat, rows, preferred_element_type=jnp.float32) * out_scale,
        )

    new_out = grown_out(out_mat, flat, upstream)
    peer_out = grown_out(jnp.concatenate(peer_mat, axis=0), peer_flat, peer_upstream)
    return (
        average(new_query, after(peer_query, peer_value))[None],
        average(new_key, after(peer_key, peer_upstream))[None],
        average(new_value, peer_value)[None],
        average(new_out, peer_out)[None],
        average(new_gain, after(peer_gain, peer_value))[None],
        input_grad[None],
    )


def per_device(
    tokens, norm_gain, w_query, key_weight, value_weight, w_out, doc_ids, upstream, step_count
):
    rounds = lax.axis_size("dp").bit_length() - 1
    which = step_count[0] % rounds
    return lax.switch(
        which,
        [functools.partial(step, 2**level) for level in range(rounds)],
        tokens[0],
        norm_gain[0],
        w_query[0],
        key_weight[0],
        value_weight[0],
        w_out[0],
        doc_ids[0],
        upstream[0],
    )


def solution(mesh):
    return jax.shard_map(
        per_device,
        mesh=mesh,
        in_specs=(
            P("dp", "tensor", None),
            P("dp", None),
            P("dp", None, "tensor"),
            P("dp", None, "tensor"),
            P("dp", None, "tensor"),
            P("dp", "tensor", None),
            P("dp", None),
            P("dp", "tensor", None),
            P(),
        ),
        out_specs=(
            P("dp", None, "tensor"),
            P("dp", None, "tensor"),
            P("dp", None, "tensor"),
            P("dp", "tensor", None),
            P("dp", None),
            P("dp", "tensor", None),
        ),
        check_vma=False,
    )
```
